32 devices in a mesh: camframe: 16 (over z, x, core), tile: 2 (over y).
Axes of the slice: x: 2, y: 2, z: 4, core: 2. Of those that a mesh axis runs over, the one named last changes fastest.
Arguments:
- latents: bfloat16 [48, 16, 8, 1280], P('camframe', 'tile'), may hold values from -6 to 6
- norm_gain: float32 [1280], replicated, may hold values from 0.1 to 1.9
- norm_shift: float32 [1280], replicated, may hold values from -3 to 3
- conv_weight: bfloat16 [3, 3, 1280, 1280], P(None, None, 'tile'), may hold values from -0.0546875 to 0.0546875
- cross_query: bfloat16 [1280, 1280], P('tile'), may hold values from -1 to 1
- cross_key: bfloat16 [1280, 1280], P('tile'), may hold values from -1 to 1
- cross_value: bfloat16 [1280, 1280], P('tile'), may hold values from -0.15625 to 0.15625
- cross_out: bfloat16 [1280, 1280], P('tile'), may hold values from -0.5 to 0.5
- time_query: bfloat16 [1280, 1280], P('tile'), may hold values from -1 to 1
- time_key: bfloat16 [1280, 1280], P('tile'), may hold values from -1 to 1
- time_value: bfloat16 [1280, 1280], P('tile'), may hold values from -0.15625 to 0.15625
- time_out: bfloat16 [1280, 1280], P('tile'), may hold values from -0.5 to 0.5
- patch_lists: int32 [6, 2, 2], replicated, may hold values from 0 to 3, as said below
- patch_counts: int32 [6, 2], replicated, may hold values from 1 to 2
Outputs:
- blended: bfloat16 [48, 16, 8, 1280], P('camframe', 'tile')
The draws below stay inside these ranges and needn't reach their ends.
Inputs may be any that keep to these rules, and one draw needn't show every extreme that they name: `patch_lists`: each camera side lists 2 different patch numbers.
All inputs are finite; a program needn't handle non-finite values.
Results may differ from the reference program's by a relative error of at most 0.025.
The reference program's roundings to bfloat16 on the way count: a program that leaves them out, or rounds other values in their place, can miss the bound.
Values may be sent and summed in bfloat16 or wider, within the bound.
A program may use at most 128 MiB of HBM per device.

```python
import jax
import jax.numpy as jnp
from jax import lax

C = 1280
HEADS = 8
GROUPS = 32
CAMS = 6
HH = 16
WW = 8
PATCH = 32
P_SIZE = 2
HEAD = 160
ITEMS = 48
FRAMES = 8
NPATCH = 4
N_TILE = 2


def draw_cross_query(key, part):
    key = jax.random.fold_in(key, 1)
    independent = jax.random.normal(key, (C, C), jnp.float32) * C ** (-0.5)
    return jnp.clip(independent, -1.0, 1.0).astype(jnp.bfloat16)


def draw_cross_key(key, part):
    key = jax.random.fold_in(key, 2)
    independent = jax.random.normal(key, (C, C), jnp.float32) * C ** (-0.5)
    return jnp.clip(independent, -1.0, 1.0).astype(jnp.bfloat16)


def draw_time_query(key, part):
    key = jax.random.fold_in(key, 3)
    independent = jax.random.normal(key, (C, C), jnp.float32) * C ** (-0.5)
    return jnp.clip(independent, -1.0, 1.0).astype(jnp.bfloat16)


def draw_time_key(key, part):
    key = jax.random.fold_in(key, 4)
    independent = jax.random.normal(key, (C, C), jnp.float32) * C ** (-0.5)
    return jnp.clip(independent, -1.0, 1.0).astype(jnp.bfloat16)


def draw_patch_lists(key, part):
    key = jax.random.fold_in(key, 5)
    score_key, pick_key = jax.random.split(key)
    scores = jax.random.randint(score_key, (CAMS * 2, NPATCH), 0, 1 << 20) * NPATCH + jnp.arange(NPATCH, dtype=jnp.int32)[None, :]
    chosen = jax.random.randint(pick_key, (), 0, CAMS * 2)
    lift_amount = jnp.where((jnp.arange(CAMS * 2)[:, None] == chosen) & (jnp.arange(NPATCH)[None, :] == NPATCH - 1), -(1 << 26), 0)
    ranking = jnp.argsort(scores + lift_amount, axis=1, stable=True)
    return ranking[:, :P_SIZE].reshape(CAMS, 2, P_SIZE).astype(jnp.int32)


def draw_patch_counts(key, part):
    key = jax.random.fold_in(key, 6)
    base_key, high_key, low_key = jax.random.split(key, 3)
    counts = jax.random.randint(base_key, (CAMS * 2,), 1, P_SIZE + 1)
    highest_place = jax.random.randint(high_key, (), 0, CAMS * 2)
    lowest_place = (highest_place + 1 + jax.random.randint(low_key, (), 0, CAMS * 2 - 1)) % (CAMS * 2)
    places = jnp.arange(CAMS * 2)
    counts = jnp.where(places == highest_place, P_SIZE, jnp.where(places == lowest_place, 1, counts))
    return counts.reshape(CAMS, 2).astype(jnp.int32)


def block_levels(own_key, shape, shards, smallest, high):
    factor_of, own = 1.0, jax.random.fold_in(own_key, 6)
    for axis_at, parts in shards:
        heights = jnp.exp(jax.random.uniform(jax.random.fold_in(own, axis_at), (parts,), jnp.float32, smallest / len(shards), high / len(shards)))
        factor_of = factor_of * jnp.repeat(heights, shape[axis_at] // parts).reshape([-1 if axis == axis_at else 1 for axis in range(len(shape))])
    return factor_of


def gaussian(own_key, shape, scale, bound, shards=(), kind=jnp.bfloat16):
    result = scale * jax.random.normal(own_key, shape, jnp.float32)
    if shards:
        result = result * block_levels(own_key, shape, shards, -0.22, 0.18)
    return jnp.clip(result, -bound, bound).astype(kind)


def setup_inputs(seed: int = 0) -> dict:
    arg_keys = jax.random.split(jax.random.key(seed), 15)
    return {
        "latents": gaussian(arg_keys[0], (ITEMS, HH, WW, C), 1.0, 6.0, ((0, 16), (1, 2))),
        "norm_gain": jnp.clip(1.0 + 0.18 * jax.random.normal(arg_keys[1], (C,), jnp.float32), 0.1, 1.9),
        "norm_shift": gaussian(arg_keys[2], (C,), 0.5, 3.0, (), jnp.float32),
        "conv_weight": gaussian(arg_keys[3], (3, 3, C, C), (9 * C) ** -0.5, 0.0546875, ((2, 2),)),
        "cross_query": draw_cross_query(jax.random.fold_in(arg_keys[14], 71), 0),
        "cross_key": draw_cross_key(jax.random.fold_in(arg_keys[14], 71), 0),
        "cross_value": gaussian(arg_keys[6], (C, C), C ** -0.5, 0.15625, ((0, 2),)),
        "cross_out": gaussian(arg_keys[7], (C, C), HEAD ** -0.5, 0.5, ((0, 2),)),
        "time_query": draw_time_query(jax.random.fold_in(arg_keys[14], 71), 0),
        "time_key": draw_time_key(jax.random.fold_in(arg_keys[14], 71), 0),
        "time_value": gaussian(arg_keys[10], (C, C), C ** -0.5, 0.15625, ((0, 2),)),
        "time_out": gaussian(arg_keys[11], (C, C), HEAD ** -0.5, 0.5, ((0, 2),)),
        "patch_lists": draw_patch_lists(jax.random.fold_in(arg_keys[14], 71), 0),
        "patch_counts": draw_patch_counts(jax.random.fold_in(arg_keys[14], 71), 0),
    }


EPSILON = 1e-05

def right_product(left, weight):
    return lax.dot_general(left, weight, (((1,), (1,)), ((), ())), preferred_element_type=jnp.float32)

def norm_silu(single_view, gain_vector, shift_vector):
    values = single_view.astype(jnp.float32)
    grouped = values.reshape(HH * WW, GROUPS, C // GROUPS)
    average = lax.optimization_barrier(jnp.mean(grouped, axis=(0, 2), keepdims=True))
    spread = lax.optimization_barrier(jnp.mean(jnp.square(grouped - average), axis=(0, 2), keepdims=True))
    normed = ((grouped - average) * lax.rsqrt(spread + EPSILON)).reshape(HH, WW, C)
    return jax.nn.silu(normed * gain_vector + shift_vector).astype(jnp.bfloat16)

def convolve(single_view, weight):
    padded = jnp.pad(single_view, ((1, 1), (1, 1), (0, 0)))
    summed = jnp.zeros((HH * WW, weight.shape[2]), jnp.float32)
    for row_shift in range(3):
        for col_shift in range(3):
            window = padded[row_shift:row_shift + HH, col_shift:col_shift + WW, :].reshape(HH * WW, C)
            summed = summed + right_product(window, weight[row_shift, col_shift])
    return summed.reshape(HH, WW, weight.shape[2])

def layer_norm(values):
    average = lax.optimization_barrier(jnp.mean(values, axis=-1, keepdims=True))
    spread = lax.optimization_barrier(jnp.mean(jnp.square(values - average), axis=-1, keepdims=True))
    return ((values - average) * lax.rsqrt(spread + EPSILON)).astype(jnp.bfloat16)

def project(single_view, weights):
    normed = layer_norm(single_view.astype(jnp.float32)).reshape(HH * WW, C)
    return tuple((right_product(normed, weight).astype(jnp.bfloat16) for weight in weights))

def grouped_out(mixture, weight):
    channels = C // N_TILE
    summed = jnp.zeros((mixture.shape[0], C), jnp.float32)
    for group_index in range(N_TILE):
        partial_sum = jnp.dot(mixture[:, group_index * channels:(group_index + 1) * channels], weight[group_index * channels:(group_index + 1) * channels], preferred_element_type=jnp.float32)
        rounded = lax.optimization_barrier(partial_sum.astype(jnp.bfloat16))
        summed = summed + rounded.astype(jnp.float32)
    return summed

def attend(queries, key_block, values, live_slots):
    tokens = queries.shape[0]
    query_heads = queries.astype(jnp.float32).reshape(tokens, HEADS, HEAD)
    key_heads = key_block.astype(jnp.float32).reshape(-1, HEADS, HEAD)
    value_heads = values.astype(jnp.float32).reshape(-1, HEADS, HEAD)
    scores = jnp.einsum('thd,lhd->htl', query_heads, key_heads, precision=lax.Precision.HIGHEST) * HEAD ** (-0.5)
    scores = jnp.where(live_slots[None, None, :], scores, -jnp.inf)
    highest = lax.optimization_barrier(jnp.max(scores, axis=-1, keepdims=True))
    weights = jnp.exp(scores - highest)
    weights = (weights / lax.optimization_barrier(jnp.sum(weights, axis=-1, keepdims=True))).astype(jnp.bfloat16)
    mixture = jnp.einsum('htl,lhd->thd', weights.astype(jnp.float32), value_heads, precision=lax.Precision.HIGHEST)
    return mixture.reshape(tokens, C).astype(jnp.bfloat16)

def reference(latents, norm_gain, norm_shift, conv_weight, cross_query, cross_key, cross_value, cross_out, time_query, time_key, time_value, time_out, patch_lists, patch_counts):
    tokens = HH * WW

    def first_part(single_view):
        activated = norm_silu(single_view, norm_gain, norm_shift)
        return (single_view.astype(jnp.float32) + convolve(activated, conv_weight)).astype(jnp.bfloat16)
    hidden = lax.map(first_part, latents)
    cross_queries, cross_keys, cross_values = lax.map(lambda single_view: project(single_view, (cross_query, cross_key, cross_value)), hidden)
    packed = jnp.concatenate([cross_keys, cross_values], axis=-1).reshape(ITEMS, NPATCH, PATCH, 2 * C)
    slot_ids = jnp.arange(P_SIZE, dtype=jnp.int32)

    def cross_view(view_index):
        camera = view_index // FRAMES
        left_view = (view_index - FRAMES) % ITEMS
        right_view = (view_index + FRAMES) % ITEMS
        left_rows = jnp.take(packed[left_view], patch_lists[camera, 0], axis=0)
        right_rows = jnp.take(packed[right_view], patch_lists[camera, 1], axis=0)
        context = jnp.concatenate([left_rows, right_rows], axis=0).reshape(2 * P_SIZE * PATCH, 2 * C)
        live_slots = jnp.concatenate([slot_ids < patch_counts[camera, 0], slot_ids < patch_counts[camera, 1]])
        live_slots = jnp.repeat(live_slots, PATCH)
        mixture = attend(cross_queries[view_index], context[:, :C], context[:, C:], live_slots)
        return grouped_out(mixture, cross_out)
    cross_total = lax.map(cross_view, jnp.arange(ITEMS, dtype=jnp.int32))
    middle = (hidden.reshape(ITEMS, tokens, C).astype(jnp.float32) + cross_total).astype(jnp.bfloat16)
    time_queries, time_keys, time_values = lax.map(lambda single_view: project(single_view, (time_query, time_key, time_value)), middle)

    def across_frames(packed_args):
        queries, key_block, values = [part_array.astype(jnp.float32).reshape(FRAMES, tokens, HEADS, HEAD) for part_array in packed_args]
        scores = jnp.einsum('fthd,gthd->thfg', queries, key_block, precision=lax.Precision.HIGHEST) * HEAD ** (-0.5)
        highest = lax.optimization_barrier(jnp.max(scores, axis=-1, keepdims=True))
        weights = jnp.exp(scores - highest)
        weights = (weights / lax.optimization_barrier(jnp.sum(weights, axis=-1, keepdims=True))).astype(jnp.bfloat16)
        mixture = jnp.einsum('thfg,gthd->fthd', weights.astype(jnp.float32), values, precision=lax.Precision.HIGHEST)
        mixture = mixture.reshape(FRAMES * tokens, C).astype(jnp.bfloat16)
        return grouped_out(mixture, time_out).reshape(FRAMES, tokens, C)
    time_total = lax.map(across_frames, (time_queries.reshape(CAMS, FRAMES, tokens, C), time_keys.reshape(CAMS, FRAMES, tokens, C), time_values.reshape(CAMS, FRAMES, tokens, C)))
    blended = (middle.astype(jnp.float32) + time_total.reshape(ITEMS, tokens, C)).astype(jnp.bfloat16)
    return blended.reshape(ITEMS, HH, WW, C)
```

```python
import functools

import jax
import jax.numpy as jnp
from jax import lax
from jax.experimental import pallas as pl
from jax.experimental.pallas import tpu as pltpu
from jax.sharding import PartitionSpec as P

GROUPS = 32
CAMS = 6
HH = 16
WW = 8
PATCH = 32
P_SIZE = 2
HEAD = 160
NPATCH = 4
TOKENS = HH * WW

EPSILON = 1e-05
MESH = pl.DeviceIdType.MESH
VMEM_BYTES = 40 * 1024 * 1024


def right_product(left, weight):
    return lax.dot_general(
        left, weight, (((1,), (1,)), ((), ())), preferred_element_type=jnp.float32
    )


def norm_silu(block_views, gain_vector, shift_vector):
    values = block_views.astype(jnp.float32)
    view_count, height, breadth, channels = values.shape
    grouped = values.reshape(view_count, height * breadth, GROUPS, channels // GROUPS)
    average = jnp.mean(grouped, axis=(1, 3), keepdims=True)
    spread = jnp.mean(jnp.square(grouped - average), axis=(1, 3), keepdims=True)
    normed = ((grouped - average) * lax.rsqrt(spread + EPSILON)).reshape(
        view_count, height, breadth, channels
    )
    return jax.nn.silu(normed * gain_vector + shift_vector).astype(jnp.bfloat16)


def convolve(activated, weight):
    return lax.conv_general_dilated(
        activated,
        weight,
        (1, 1),
        ((1, 1), (1, 1)),
        dimension_numbers=("NHWC", "HWOI", "NHWC"),
        preferred_element_type=jnp.float32,
    )


def layer_norm(values):
    average = jnp.mean(values, axis=-1, keepdims=True)
    centred = values - average
    spread = jnp.mean(jnp.square(centred), axis=-1, keepdims=True)
    return (centred * lax.rsqrt(spread + EPSILON)).astype(jnp.bfloat16)


def head_windows(width):
    windows = []
    for head in range(width // HEAD):
        first, last = head * HEAD, (head + 1) * HEAD
        low = first // 128 * 128
        high = min(width, -(-last // 128) * 128)
        windows.append((first, last, low, high))
    return windows


def masked_attention(queries, keys, values, keep, mixture):
    width = queries.shape[1]
    mixture[...] = jnp.zeros_like(mixture)
    for first, last, low, high in head_windows(width):
        lane = lax.broadcasted_iota(jnp.int32, (1, high - low), 1) + low
        inside = (lane >= first) & (lane < last)
        own_queries = jnp.where(inside, queries[:, low:high], jnp.bfloat16(0))
        own_values = jnp.where(inside, values[:, low:high], jnp.bfloat16(0))
        scores = right_product(own_queries, keys[:, low:high]) * HEAD ** (-0.5)
        scores = jnp.where(keep, scores, -jnp.inf)
        highest = jnp.max(scores, axis=-1, keepdims=True)
        weights = jnp.exp(scores - highest)
        weights = (weights / jnp.sum(weights, axis=-1, keepdims=True)).astype(jnp.bfloat16)
        mixture[:, low:high] += jnp.dot(
            weights, own_values, preferred_element_type=jnp.float32
        )
    return mixture[...].astype(jnp.bfloat16)


def cross_kernel(
    cycle, tiles, lists_ref, counts_ref, hidden_ref, wq_ref, wk_ref, wv_ref, wo_ref,
    middle_ref,
    query_buf, kv_buf, send_buf, context, part, arrived, mixture,
    kv_send, kv_recv, rs_send, rs_recv, ag_send, ag_recv,
):
    per_device, _, rows, channels = hidden_ref.shape
    width = wq_ref.shape[0]
    views = per_device * cycle
    frames = views // CAMS
    me = lax.axis_index("camframe")
    tile = lax.axis_index("tile")
    steps = [(side, position, (frames, -frames)[side]) for side in range(2) for position in range(per_device)]
    offsets = sorted({((position + step) // per_device) % cycle for _, position, step in steps})
    barrier = pltpu.get_barrier_semaphore()
    for offset in offsets:
        pl.semaphore_signal(
            barrier, inc=1, device_id=(lax.rem(me + offset, cycle), tile), device_id_type=MESH
        )
    for other in range(1, tiles):
        pl.semaphore_signal(
            barrier, inc=1, device_id=(me, lax.rem(tile + other, tiles)), device_id_type=MESH
        )

    normed = layer_norm(
        hidden_ref[...].reshape(per_device * TOKENS, channels).astype(jnp.float32)
    )
    block = (per_device, NPATCH, PATCH, width)
    kv_buf[:, :, 0] = right_product(normed, wk_ref[...]).astype(jnp.bfloat16).reshape(block)
    kv_buf[:, :, 1] = right_product(normed, wv_ref[...]).astype(jnp.bfloat16).reshape(block)
    pl.semaphore_wait(barrier, len(offsets) + tiles - 1)
    copies = {}
    for side, position, step in steps:
        target_view = lax.rem(per_device * me + position + step + views, views)
        camera = target_view // frames
        for slot in range(P_SIZE):
            chosen = lists_ref[(camera * 2 + side) * P_SIZE + slot]
            send_buf[position, side, slot] = kv_buf[position, chosen]
        target = lax.rem(me + ((position + step) // per_device) % cycle, cycle)
        target_slot = (position + step) % per_device
        copy = pltpu.make_async_remote_copy(
            src_ref=send_buf.at[position, side],
            dst_ref=context.at[target_slot, side],
            send_sem=kv_send.at[position, side],
            recv_sem=kv_recv.at[target_slot, side],
            device_id=(target, tile),
            device_id_type=MESH,
        )
        copy.start()
        copies[target_slot, side] = copy
    query_buf[...] = (
        right_product(normed, wq_ref[...]).astype(jnp.bfloat16).reshape(query_buf.shape)
    )

    def attend(position):
        copies[position, 0].wait_recv()
        copies[position, 1].wait_recv()
        camera = (per_device * me + position) // frames
        place = lax.broadcasted_iota(jnp.int32, (1, 2 * P_SIZE * PATCH), 1) // PATCH
        count = jnp.where(
            place < P_SIZE, counts_ref[camera * 2], counts_ref[camera * 2 + 1]
        )
        keep = lax.rem(place, P_SIZE) < count
        keys = context[position, :, :, 0].reshape(2 * P_SIZE * PATCH, width)
        values = context[position, :, :, 1].reshape(2 * P_SIZE * PATCH, width)
        mixed = masked_attention(query_buf[position], keys, values, keep, mixture)
        total = jnp.dot(mixed, wo_ref[...], preferred_element_type=jnp.float32)
        part[position] = total.astype(jnp.bfloat16).reshape(tiles, rows, channels)
        return scatter(me, tile, tiles, position, part, arrived, rs_send, rs_recv)

    def finish(position, sent):
        total = gather_sum(tile, tiles, position, part, arrived, sent)
        own = hidden_ref[position, tile].astype(jnp.float32) + total
        middle_ref[position, tile] = own.astype(jnp.bfloat16)
        started = []
        for other in range(1, tiles):
            target = lax.rem(tile + other, tiles)
            copy = pltpu.make_async_remote_copy(
                src_ref=middle_ref.at[position, tile],
                dst_ref=middle_ref.at[position, tile],
                send_sem=ag_send.at[position, other],
                recv_sem=ag_recv.at[position, other],
                device_id=(me, target),
                device_id_type=MESH,
            )
            copy.start()
            started.append(copy)
        return started

    pending, started = None, []
    for position in range(per_device):
        sent = attend(position)
        if pending is not None:
            started += finish(*pending)
        pending = (position, sent)
    started += finish(*pending)
    for copy in started:
        copy.wait()
    for copy in copies.values():
        copy.wait_send()


def scatter(me, tile, tiles, position, part, arrived, send_sem, recv_sem):
    started = []
    for other in range(1, tiles):
        target = lax.rem(tile + other, tiles)
        copy = pltpu.make_async_remote_copy(
            src_ref=part.at[position, target],
            dst_ref=arrived.at[position, other],
            send_sem=send_sem.at[position, other],
            recv_sem=recv_sem.at[position, other],
            device_id=(me, target),
            device_id_type=MESH,
        )
        copy.start()
        started.append(copy)
    return started


def gather_sum(tile, tiles, position, part, arrived, sent):
    for copy in sent:
        copy.wait()
    total = part[position, tile].astype(jnp.float32)
    for other in range(1, tiles):
        total = total + arrived[position, other].astype(jnp.float32)
    return total


def time_kernel(
    cycle, tiles, middle_ref, wq_ref, wk_ref, wv_ref, wo_ref,
    out_ref,
    local, received, mixed, returned, part, arrived, mixture,
    qkv_send, qkv_recv, mix_send, mix_recv, rs_send, rs_recv,
):
    per_device, _, rows, channels = middle_ref.shape
    width = wq_ref.shape[0]
    frames = per_device * cycle // CAMS
    cells = TOKENS // frames
    me = lax.axis_index("camframe")
    tile = lax.axis_index("tile")
    first_camera = per_device * me // frames
    last_camera = (per_device * me + per_device - 1) // frames
    reach = (frames - 1 + per_device - 1) // per_device
    barrier = pltpu.get_barrier_semaphore()

    def is_peer(offset):
        other = me + offset
        other_first = (per_device * (other + cycle)) // frames - CAMS
        other_last = (per_device * (other + cycle) + per_device - 1) // frames - CAMS
        return (other >= 0) & (other < cycle) & (other_first <= last_camera) & (first_camera <= other_last)

    for offset in range(-reach, reach + 1):
        if offset != 0:
            @pl.when(is_peer(offset))
            def _():
                pl.semaphore_signal(
                    barrier, inc=1, device_id=(me + offset, tile), device_id_type=MESH
                )
    for other in range(1, tiles):
        pl.semaphore_signal(
            barrier, inc=1, device_id=(me, lax.rem(tile + other, tiles)), device_id_type=MESH
        )

    normed = layer_norm(
        middle_ref[...].reshape(per_device * TOKENS, channels).astype(jnp.float32)
    )
    for which, weight_ref in enumerate((wq_ref, wk_ref, wv_ref)):
        local[:, :, which] = (
            right_product(normed, weight_ref[...])
            .astype(jnp.bfloat16)
            .reshape(per_device, frames, cells, width)
        )
    peers = tiles - 1
    for offset in range(-reach, reach + 1):
        if offset != 0:
            peers = peers + jnp.where(is_peer(offset), 1, 0)
    pl.semaphore_wait(barrier, peers)

    def transpose(source, target, send_sem, recv_sem, slot, group, action):
        unit = per_device * me + slot
        camera, frame = unit // frames, lax.rem(unit, frames)
        goal = camera * frames + group
        goal_device, goal_slot = goal // per_device, lax.rem(goal, per_device)
        remote = pltpu.make_async_remote_copy(
            src_ref=source.at[slot, group],
            dst_ref=target.at[goal_slot, frame],
            send_sem=send_sem.at[slot, group],
            recv_sem=recv_sem.at[goal_slot, frame],
            device_id=(goal_device, tile),
            device_id_type=MESH,
        )
        if action == "start":
            @pl.when(goal_device != me)
            def _():
                remote.start()

            @pl.when(goal_device == me)
            def _():
                pltpu.make_async_copy(
                    source.at[slot, group], target.at[goal_slot, frame], recv_sem.at[goal_slot, frame]
                ).start()
        else:
            @pl.when(goal_device != me)
            def _():
                remote.wait_send()

    def landed(source, target, recv_sem, slot, frame):
        pltpu.make_async_copy(
            source.at[slot, frame], target.at[slot, frame], recv_sem.at[slot, frame]
        ).wait()

    def each(slot, action):
        def body(group, carry):
            action(slot, group)
            return carry

        lax.fori_loop(0, frames, body, 0)

    for slot in range(per_device):
        each(slot, lambda s, g: transpose(local, received, qkv_send, qkv_recv, s, g, "start"))
    tokens_in = frames * cells
    row_cell = lax.rem(lax.broadcasted_iota(jnp.int32, (tokens_in, tokens_in), 0), cells)
    column_cell = lax.rem(lax.broadcasted_iota(jnp.int32, (tokens_in, tokens_in), 1), cells)
    keep = row_cell == column_cell
    for slot in range(per_device):
        each(slot, lambda s, g: landed(local, received, qkv_recv, s, g))
        queries, keys, values = (
            received[slot, :, which].reshape(tokens_in, width) for which in range(3)
        )
        result = masked_attention(queries, keys, values, keep, mixture)
        mixed[slot] = result.reshape(frames, cells, width)
        each(slot, lambda s, g: transpose(mixed, returned, mix_send, mix_recv, s, g, "start"))
    sent = []
    for slot in range(per_device):
        each(slot, lambda s, g: landed(mixed, returned, mix_recv, s, g))
        total = jnp.dot(
            returned[slot].reshape(TOKENS, width), wo_ref[...], preferred_element_type=jnp.float32
        )
        part[slot] = total.astype(jnp.bfloat16).reshape(tiles, rows, channels)
        sent.append(scatter(me, tile, tiles, slot, part, arrived, rs_send, rs_recv))
    for slot in range(per_device):
        total = gather_sum(tile, tiles, slot, part, arrived, sent[slot])
        own = middle_ref[slot, tile].astype(jnp.float32) + total
        out_ref[slot] = own.astype(jnp.bfloat16)
    for slot in range(per_device):
        each(slot, lambda s, g: transpose(local, received, qkv_send, qkv_recv, s, g, "wait"))
        each(slot, lambda s, g: transpose(mixed, returned, mix_send, mix_recv, s, g, "wait"))


def vmem(count):
    return [pl.BlockSpec(memory_space=pltpu.VMEM)] * count


def cross_block(cycle, tiles, lists, counts, hidden, wq, wk, wv, wo):
    per_device, _, rows, channels = hidden.shape
    width = wq.shape[0]
    kind = jnp.bfloat16
    dma = pltpu.SemaphoreType.DMA
    return pl.pallas_call(
        functools.partial(cross_kernel, cycle, tiles),
        out_shape=jax.ShapeDtypeStruct(hidden.shape, kind),
        in_specs=[pl.BlockSpec(memory_space=pltpu.SMEM)] * 2 + vmem(5),
        out_specs=pl.BlockSpec(memory_space=pltpu.VMEM),
        scratch_shapes=[
            pltpu.VMEM((per_device, TOKENS, width), kind),
            pltpu.VMEM((per_device, NPATCH, 2, PATCH, width), kind),
            pltpu.VMEM((per_device, 2, P_SIZE, 2, PATCH, width), kind),
            pltpu.VMEM((per_device, 2, P_SIZE, 2, PATCH, width), kind),
            pltpu.VMEM((per_device, tiles, rows, channels), kind),
            pltpu.VMEM((per_device, tiles, rows, channels), kind),
            pltpu.VMEM((TOKENS, width), jnp.float32),
            dma((per_device, 2)),
            dma((per_device, 2)),
            dma((per_device, tiles)),
            dma((per_device, tiles)),
            dma((per_device, tiles)),
            dma((per_device, tiles)),
        ],
        compiler_params=pltpu.CompilerParams(
            collective_id=1, has_side_effects=True, vmem_limit_bytes=VMEM_BYTES
        ),
        name="cross_block",
    )(lists.reshape(-1), counts.reshape(-1), hidden, wq, wk, wv, wo)


def time_block(cycle, tiles, middle, wq, wk, wv, wo):
    per_device, _, rows, channels = middle.shape
    width = wq.shape[0]
    frames = per_device * cycle // CAMS
    cells = TOKENS // frames
    kind = jnp.bfloat16
    dma = pltpu.SemaphoreType.DMA
    return pl.pallas_call(
        functools.partial(time_kernel, cycle, tiles),
        out_shape=jax.ShapeDtypeStruct((per_device, rows, channels), kind),
        in_specs=vmem(5),
        out_specs=pl.BlockSpec(memory_space=pltpu.VMEM),
        scratch_shapes=[
            pltpu.VMEM((per_device, frames, 3, cells, width), kind),
            pltpu.VMEM((per_device, frames, 3, cells, width), kind),
            pltpu.VMEM((per_device, frames, cells, width), kind),
            pltpu.VMEM((per_device, frames, cells, width), kind),
            pltpu.VMEM((per_device, tiles, rows, channels), kind),
            pltpu.VMEM((per_device, tiles, rows, channels), kind),
            pltpu.VMEM((frames * cells, width), jnp.float32),
            dma((per_device, frames)),
            dma((per_device, frames)),
            dma((per_device, frames)),
            dma((per_device, frames)),
            dma((per_device, tiles)),
            dma((per_device, tiles)),
        ],
        compiler_params=pltpu.CompilerParams(
            collective_id=2, has_side_effects=True, vmem_limit_bytes=VMEM_BYTES
        ),
        name="time_block",
    )(middle, wq, wk, wv, wo)


def on_device(
    latents, norm_gain, norm_shift, conv_weight,
    cross_query, cross_key, cross_value, cross_out,
    time_query, time_key, time_value, time_out,
    patch_lists, patch_counts,
):
    per_device, share_rows = latents.shape[:2]
    channels = latents.shape[3]
    cycle = lax.axis_size("camframe")
    tiles = lax.axis_size("tile")
    tile_index = lax.axis_index("tile")
    local_width = conv_weight.shape[2]
    whole_views = lax.all_gather(latents, "tile", axis=1, tiled=True)
    activated = norm_silu(whole_views, norm_gain, norm_shift)
    residual_part = lax.dynamic_slice_in_dim(
        whole_views, tile_index * local_width, local_width, 3
    ).astype(jnp.float32)
    own_hidden = (residual_part + convolve(activated, conv_weight)).astype(jnp.bfloat16)
    hidden = lax.all_gather(own_hidden, "tile", axis=3, tiled=True)
    hidden = hidden.reshape(per_device, tiles, share_rows * WW, channels)
    middle = cross_block(
        cycle, tiles, patch_lists, patch_counts, hidden,
        cross_query, cross_key, cross_value, cross_out,
    )
    blended = time_block(cycle, tiles, middle, time_query, time_key, time_value, time_out)
    return blended.reshape(latents.shape)


def solution(mesh):
    return jax.shard_map(
        on_device,
        mesh=mesh,
        in_specs=(
            P("camframe", "tile", None, None),
            P(),
            P(),
            P(None, None, "tile", None),
            P("tile", None),
            P("tile", None),
            P("tile", None),
            P("tile", None),
            P("tile", None),
            P("tile", None),
            P("tile", None),
            P("tile", None),
            P(),
            P(),
        ),
        out_specs=P("camframe", "tile", None, None),
        check_vma=False,
    )
```

```python
import functools

import jax
import jax.numpy as jnp
from jax import lax
from jax.experimental import pallas as pl
from jax.experimental.pallas import tpu as pltpu
from jax.sharding import PartitionSpec as P

GROUPS = 32
CAMS = 6
HH = 16
WW = 8
PATCH = 32
P_SIZE = 2
HEAD = 160
NPATCH = 4
TOKENS = HH * WW

EPSILON = 1e-05
MESH = pl.DeviceIdType.MESH
VMEM_BYTES = 40 * 1024 * 1024


def right_product(left, weight):
    return lax.dot_general(
        left, weight, (((1,), (1,)), ((), ())), preferred_element_type=jnp.float32
    )


def layer_norm(values):
    average = jnp.mean(values, axis=-1, keepdims=True)
    centred = values - average
    spread = jnp.mean(jnp.square(centred), axis=-1, keepdims=True)
    return (centred * lax.rsqrt(spread + EPSILON)).astype(jnp.bfloat16)


def head_windows(width):
    windows = []
    for head in range(width // HEAD):
        first, last = head * HEAD, (head + 1) * HEAD
        low = first // 128 * 128
        high = min(width, -(-last // 128) * 128)
        windows.append((first, last, low, high))
    return windows


def masked_attention(queries, keys, values, keep, mixture):
    width = queries.shape[1]
    mixture[...] = jnp.zeros_like(mixture)
    for first, last, low, high in head_windows(width):
        lane = lax.broadcasted_iota(jnp.int32, (1, high - low), 1) + low
        inside = (lane >= first) & (lane < last)
        own_queries = jnp.where(inside, queries[:, low:high], jnp.bfloat16(0))
        own_values = jnp.where(inside, values[:, low:high], jnp.bfloat16(0))
        scores = right_product(own_queries, keys[:, low:high]) * HEAD ** (-0.5)
        scores = jnp.where(keep, scores, -jnp.inf)
        highest = jnp.max(scores, axis=-1, keepdims=True)
        weights = jnp.exp(scores - highest)
        weights = (weights / jnp.sum(weights, axis=-1, keepdims=True)).astype(jnp.bfloat16)
        mixture[:, low:high] += jnp.dot(
            weights, own_values, preferred_element_type=jnp.float32
        )
    return mixture[...].astype(jnp.bfloat16)


def cross_kernel(
    cycle, tiles, lists_ref, counts_ref, hidden_ref, wq_ref, wk_ref, wv_ref, wo_ref,
    middle_ref,
    query_buf, kv_buf, send_buf, context, part, arrived, mixture,
    kv_send, kv_recv, rs_send, rs_recv, ag_send, ag_recv,
):
    per_device, _, rows, channels = hidden_ref.shape
    width = wq_ref.shape[0]
    views = per_device * cycle
    frames = views // CAMS
    me = lax.axis_index("camframe")
    tile = lax.axis_index("tile")
    steps = [(side, position, (frames, -frames)[side]) for side in range(2) for position in range(per_device)]
    offsets = sorted({((position + step) // per_device) % cycle for _, position, step in steps})
    barrier = pltpu.get_barrier_semaphore()
    for offset in offsets:
        pl.semaphore_signal(
            barrier, inc=1, device_id=(lax.rem(me + offset, cycle), tile), device_id_type=MESH
        )
    for other in range(1, tiles):
        pl.semaphore_signal(
            barrier, inc=1, device_id=(me, lax.rem(tile + other, tiles)), device_id_type=MESH
        )

    normed = layer_norm(
        hidden_ref[...].reshape(per_device * TOKENS, channels).astype(jnp.float32)
    )
    block = (per_device, NPATCH, PATCH, width)
    kv_buf[:, :, 0] = right_product(normed, wk_ref[...]).astype(jnp.bfloat16).reshape(block)
    kv_buf[:, :, 1] = right_product(normed, wv_ref[...]).astype(jnp.bfloat16).reshape(block)
    pl.semaphore_wait(barrier, len(offsets) + tiles - 1)
    copies = {}
    for side, position, step in steps:
        target_view = lax.rem(per_device * me + position + step + views, views)
        camera = target_view // frames
        for slot in range(P_SIZE):
            chosen = lists_ref[(camera * 2 + side) * P_SIZE + slot]
            send_buf[position, side, slot] = kv_buf[position, chosen]
        target = lax.rem(me + ((position + step) // per_device) % cycle, cycle)
        target_slot = (position + step) % per_device
        copy = pltpu.make_async_remote_copy(
            src_ref=send_buf.at[position, side],
            dst_ref=context.at[target_slot, side],
            send_sem=kv_send.at[position, side],
            recv_sem=kv_recv.at[target_slot, side],
            device_id=(target, tile),
            device_id_type=MESH,
        )
        copy.start()
        copies[target_slot, side] = copy
    query_buf[...] = (
        right_product(normed, wq_ref[...]).astype(jnp.bfloat16).reshape(query_buf.shape)
    )

    def attend(position):
        copies[position, 0].wait_recv()
        copies[position, 1].wait_recv()
        camera = (per_device * me + position) // frames
        place = lax.broadcasted_iota(jnp.int32, (1, 2 * P_SIZE * PATCH), 1) // PATCH
        count = jnp.where(
            place < P_SIZE, counts_ref[camera * 2], counts_ref[camera * 2 + 1]
        )
        keep = lax.rem(place, P_SIZE) < count
        keys = context[position, :, :, 0].reshape(2 * P_SIZE * PATCH, width)
        values = context[position, :, :, 1].reshape(2 * P_SIZE * PATCH, width)
        mixed = masked_attention(query_buf[position], keys, values, keep, mixture)
        total = jnp.dot(mixed, wo_ref[...], preferred_element_type=jnp.float32)
        part[position] = total.astype(jnp.bfloat16).reshape(tiles, rows, channels)
        return scatter(me, tile, tiles, position, part, arrived, rs_send, rs_recv)

    def finish(position, sent):
        total = gather_sum(tile, tiles, position, part, arrived, sent)
        own = hidden_ref[position, tile].astype(jnp.float32) + total
        middle_ref[position, tile] = own.astype(jnp.bfloat16)
        started = []
        for other in range(1, tiles):
            target = lax.rem(tile + other, tiles)
            copy = pltpu.make_async_remote_copy(
                src_ref=middle_ref.at[position, tile],
                dst_ref=middle_ref.at[position, tile],
                send_sem=ag_send.at[position, other],
                recv_sem=ag_recv.at[position, other],
                device_id=(me, target),
                device_id_type=MESH,
            )
            copy.start()
            started.append(copy)
        return started

    pending, started = None, []
    for position in range(per_device):
        sent = attend(position)
        if pending is not None:
            started += finish(*pending)
        pending = (position, sent)
    started += finish(*pending)
    for copy in started:
        copy.wait()
    for copy in copies.values():
        copy.wait_send()


def scatter(me, tile, tiles, position, part, arrived, send_sem, recv_sem):
    started = []
    for other in range(1, tiles):
        target = lax.rem(tile + other, tiles)
        copy = pltpu.make_async_remote_copy(
            src_ref=part.at[position, target],
            dst_ref=arrived.at[position, other],
            send_sem=send_sem.at[position, other],
            recv_sem=recv_sem.at[position, other],
            device_id=(me, target),
            device_id_type=MESH,
        )
        copy.start()
        started.append(copy)
    return started


def gather_sum(tile, tiles, position, part, arrived, sent):
    for copy in sent:
        copy.wait()
    total = part[position, tile].astype(jnp.float32)
    for other in range(1, tiles):
        total = total + arrived[position, other].astype(jnp.float32)
    return total


def time_kernel(
    cycle, tiles, middle_ref, wq_ref, wk_ref, wv_ref, wo_ref,
    out_ref,
    local, received, mixed, returned, part, arrived, mixture,
    qkv_send, qkv_recv, mix_send, mix_recv, rs_send, rs_recv,
):
    per_device, _, rows, channels = middle_ref.shape
    width = wq_ref.shape[0]
    frames = per_device * cycle // CAMS
    cells = TOKENS // frames
    me = lax.axis_index("camframe")
    tile = lax.axis_index("tile")
    first_camera = per_device * me // frames
    last_camera = (per_device * me + per_device - 1) // frames
    reach = (frames - 1 + per_device - 1) // per_device
    barrier = pltpu.get_barrier_semaphore()

    def is_peer(offset):
        other = me + offset
        other_first = (per_device * (other + cycle)) // frames - CAMS
        other_last = (per_device * (other + cycle) + per_device - 1) // frames - CAMS
        return (other >= 0) & (other < cycle) & (other_first <= last_camera) & (first_camera <= other_last)

    for offset in range(-reach, reach + 1):
        if offset != 0:
            @pl.when(is_peer(offset))
            def _():
                pl.semaphore_signal(
                    barrier, inc=1, device_id=(me + offset, tile), device_id_type=MESH
                )
    for other in range(1, tiles):
        pl.semaphore_signal(
            barrier, inc=1, device_id=(me, lax.rem(tile + other, tiles)), device_id_type=MESH
        )

    normed = layer_norm(
        middle_ref[...].reshape(per_device * TOKENS, channels).astype(jnp.float32)
    )
    for which, weight_ref in enumerate((wq_ref, wk_ref, wv_ref)):
        local[:, :, which] = (
            right_product(normed, weight_ref[...])
            .astype(jnp.bfloat16)
            .reshape(per_device, frames, cells, width)
        )
    peers = tiles - 1
    for offset in range(-reach, reach + 1):
        if offset != 0:
            peers = peers + jnp.where(is_peer(offset), 1, 0)
    pl.semaphore_wait(barrier, peers)

    def transpose(source, target, send_sem, recv_sem, slot, group, action):
        unit = per_device * me + slot
        camera, frame = unit // frames, lax.rem(unit, frames)
        goal = camera * frames + group
        goal_device, goal_slot = goal // per_device, lax.rem(goal, per_device)
        remote = pltpu.make_async_remote_copy(
            src_ref=source.at[slot, group],
            dst_ref=target.at[goal_slot, frame],
            send_sem=send_sem.at[slot, group],
            recv_sem=recv_sem.at[goal_slot, frame],
            device_id=(goal_device, tile),
            device_id_type=MESH,
        )
        if action == "start":
            @pl.when(goal_device != me)
            def _():
                remote.start()

            @pl.when(goal_device == me)
            def _():
                pltpu.make_async_copy(
                    source.at[slot, group], target.at[goal_slot, frame], recv_sem.at[goal_slot, frame]
                ).start()
        else:
            @pl.when(goal_device != me)
            def _():
                remote.wait_send()

    def landed(source, target, recv_sem, slot, frame):
        pltpu.make_async_copy(
            source.at[slot, frame], target.at[slot, frame], recv_sem.at[slot, frame]
        ).wait()

    def each(slot, action):
        def body(group, carry):
            action(slot, group)
            return carry

        lax.fori_loop(0, frames, body, 0)

    for slot in range(per_device):
        each(slot, lambda s, g: transpose(local, received, qkv_send, qkv_recv, s, g, "start"))
    tokens_in = frames * cells
    row_cell = lax.rem(lax.broadcasted_iota(jnp.int32, (tokens_in, tokens_in), 0), cells)
    column_cell = lax.rem(lax.broadcasted_iota(jnp.int32, (tokens_in, tokens_in), 1), cells)
    keep = row_cell == column_cell
    for slot in range(per_device):
        each(slot, lambda s, g: landed(local, received, qkv_recv, s, g))
        queries, keys, values = (
            received[slot, :, which].reshape(tokens_in, width) for which in range(3)
        )
        result = masked_attention(queries, keys, values, keep, mixture)
        mixed[slot] = result.reshape(frames, cells, width)
        each(slot, lambda s, g: transpose(mixed, returned, mix_send, mix_recv, s, g, "start"))
    sent = []
    for slot in range(per_device):
        each(slot, lambda s, g: landed(mixed, returned, mix_recv, s, g))
        total = jnp.dot(
            returned[slot].reshape(TOKENS, width), wo_ref[...], preferred_element_type=jnp.float32
        )
        part[slot] = total.astype(jnp.bfloat16).reshape(tiles, rows, channels)
        sent.append(scatter(me, tile, tiles, slot, part, arrived, rs_send, rs_recv))
    for slot in range(per_device):
        total = gather_sum(tile, tiles, slot, part, arrived, sent[slot])
        own = middle_ref[slot, tile].astype(jnp.float32) + total
        out_ref[slot] = own.astype(jnp.bfloat16)
    for slot in range(per_device):
        each(slot, lambda s, g: transpose(local, received, qkv_send, qkv_recv, s, g, "wait"))
        each(slot, lambda s, g: transpose(mixed, returned, mix_send, mix_recv, s, g, "wait"))


def vmem(count):
    return [pl.BlockSpec(memory_space=pltpu.VMEM)] * count


def group_sums(row, members):
    high = row.astype(jnp.bfloat16).astype(jnp.float32)
    middle = (row - high).astype(jnp.bfloat16).astype(jnp.float32)
    low = row - high - middle
    place = lax.broadcasted_iota(jnp.int32, (16, row.shape[1]), 0)
    parts = jnp.where(
        place == 0, high, jnp.where(place == 1, middle, jnp.where(place == 2, low, 0.0))
    ).astype(jnp.bfloat16)
    sums = jnp.dot(parts, members, preferred_element_type=jnp.float32)
    return jnp.sum(sums, axis=0, keepdims=True)


def conv_kernel(
    tiles, latents_ref, gain_ref, shift_ref, weight_ref,
    hidden_ref,
    whole, windows, weights, gathered, total,
    weight_sem, in_send, in_recv, out_send, out_recv,
):
    per_device, rows, channels = latents_ref.shape
    width = weight_ref.shape[1]
    me = lax.axis_index("camframe")
    tile = lax.axis_index("tile")
    taps = weight_ref.shape[0]

    def load(tap):
        return pltpu.make_async_copy(weight_ref.at[tap], weights.at[tap], weight_sem.at[tap])

    for tap in range(taps):
        load(tap).start()
    barrier = pltpu.get_barrier_semaphore()
    for other in range(1, tiles):
        pl.semaphore_signal(
            barrier, inc=1, device_id=(me, lax.rem(tile + other, tiles)), device_id_type=MESH
        )
    pl.semaphore_wait(barrier, tiles - 1)

    def to_others(source, target, send_sem, recv_sem, position):
        started = []
        for other in range(1, tiles):
            copy = pltpu.make_async_remote_copy(
                src_ref=source,
                dst_ref=target,
                send_sem=send_sem.at[position, other],
                recv_sem=recv_sem.at[position, other],
                device_id=(me, lax.rem(tile + other, tiles)),
                device_id_type=MESH,
            )
            copy.start()
            started.append(copy)
        return started

    incoming = [
        to_others(
            latents_ref.at[position], whole.at[position, tile], in_send, in_recv, position
        )
        for position in range(per_device)
    ]
    size = channels // GROUPS
    shape = (channels, 128)
    members = (
        lax.broadcasted_iota(jnp.int32, shape, 0) // size
        == lax.broadcasted_iota(jnp.int32, shape, 1)
    ).astype(jnp.float32).astype(jnp.bfloat16)
    shape = (128, channels)
    spread_out = (
        lax.broadcasted_iota(jnp.int32, shape, 1) // size
        == lax.broadcasted_iota(jnp.int32, shape, 0)
    ).astype(jnp.float32).astype(jnp.bfloat16)
    column = lax.rem(lax.broadcasted_iota(jnp.int32, (TOKENS, 1), 0), WW)

    def group_mean(row):
        return group_sums(group_sums(row, members) / size, spread_out)

    def prepare(position):
        whole[position, tile] = latents_ref[position]
        for copy in incoming[position]:
            copy.wait()
        values = whole[position].reshape(TOKENS, channels).astype(jnp.float32)
        channel_mean = jnp.mean(values, axis=0, keepdims=True)
        average = group_mean(channel_mean)
        centred = values - average
        spread = group_mean(jnp.mean(jnp.square(centred), axis=0, keepdims=True))
        normed = centred * lax.rsqrt(spread + EPSILON)
        activated = jax.nn.silu(normed * gain_ref[...] + shift_ref[...])
        empty_row = jnp.zeros((1, channels), jnp.float32)
        empty = jnp.zeros((WW, channels), jnp.float32)
        for col_shift in range(3):
            if col_shift == 0:
                moved = jnp.concatenate([empty_row, activated[:-1]], axis=0)
                moved = jnp.where(column == 0, 0.0, moved)
            elif col_shift == 2:
                moved = jnp.concatenate([activated[1:], empty_row], axis=0)
                moved = jnp.where(column == WW - 1, 0.0, moved)
            else:
                moved = activated
            windows[position, col_shift] = jnp.concatenate(
                [empty, moved[:-WW]], axis=0
            ).astype(jnp.bfloat16)
            windows[position, 3 + col_shift] = moved.astype(jnp.bfloat16)
            windows[position, 6 + col_shift] = jnp.concatenate(
                [moved[WW:], empty], axis=0
            ).astype(jnp.bfloat16)

    outgoing = []
    for position in range(per_device):
        prepare(position)
        total[...] = jnp.zeros_like(total)

        def add(tap, carry):
            if position == 0:
                load(tap).wait()
            total[...] += right_product(windows[position, tap], weights[tap])
            return carry

        lax.fori_loop(0, taps, add, 0)
        residual = jnp.zeros((TOKENS, width), jnp.float32)
        for part in range(tiles):
            share = whole[position, :, :, part * width : (part + 1) * width]
            share = share.reshape(TOKENS, width).astype(jnp.float32)
            residual = jnp.where(tile == part, share, residual)
        gathered[position, tile] = (residual + total[...]).astype(jnp.bfloat16)
        outgoing.append(
            to_others(
                gathered.at[position, tile], gathered.at[position, tile],
                out_send, out_recv, position,
            )
        )
    for position in range(per_device):
        for copy in outgoing[position]:
            copy.wait()
        for part in range(tiles):
            hidden_ref[position, :, part * width : (part + 1) * width] = gathered[position, part]


def conv_block(tiles, latents, gain, shift, weight):
    per_device, rows, channels = latents.shape
    taps, width = weight.shape[:2]
    kind = jnp.bfloat16
    dma = pltpu.SemaphoreType.DMA
    return pl.pallas_call(
        functools.partial(conv_kernel, tiles),
        out_shape=jax.ShapeDtypeStruct((per_device, TOKENS, channels), kind),
        in_specs=vmem(3) + [pl.BlockSpec(memory_space=pl.ANY)],
        out_specs=pl.BlockSpec(memory_space=pltpu.VMEM),
        scratch_shapes=[
            pltpu.VMEM((per_device, tiles, rows, channels), kind),
            pltpu.VMEM((per_device, taps, TOKENS, channels), kind),
            pltpu.VMEM((taps, width, channels), kind),
            pltpu.VMEM((per_device, tiles, TOKENS, width), kind),
            pltpu.VMEM((TOKENS, width), jnp.float32),
            dma((taps,)),
            dma((per_device, tiles)),
            dma((per_device, tiles)),
            dma((per_device, tiles)),
            dma((per_device, tiles)),
        ],
        compiler_params=pltpu.CompilerParams(
            collective_id=3, has_side_effects=True, vmem_limit_bytes=VMEM_BYTES
        ),
        name="conv_block",
    )(latents, gain, shift, weight)


def cross_block(cycle, tiles, lists, counts, hidden, wq, wk, wv, wo):
    per_device, _, rows, channels = hidden.shape
    width = wq.shape[0]
    kind = jnp.bfloat16
    dma = pltpu.SemaphoreType.DMA
    return pl.pallas_call(
        functools.partial(cross_kernel, cycle, tiles),
        out_shape=jax.ShapeDtypeStruct(hidden.shape, kind),
        in_specs=[pl.BlockSpec(memory_space=pltpu.SMEM)] * 2 + vmem(5),
        out_specs=pl.BlockSpec(memory_space=pltpu.VMEM),
        scratch_shapes=[
            pltpu.VMEM((per_device, TOKENS, width), kind),
            pltpu.VMEM((per_device, NPATCH, 2, PATCH, width), kind),
            pltpu.VMEM((per_device, 2, P_SIZE, 2, PATCH, width), kind),
            pltpu.VMEM((per_device, 2, P_SIZE, 2, PATCH, width), kind),
            pltpu.VMEM((per_device, tiles, rows, channels), kind),
            pltpu.VMEM((per_device, tiles, rows, channels), kind),
            pltpu.VMEM((TOKENS, width), jnp.float32),
            dma((per_device, 2)),
            dma((per_device, 2)),
            dma((per_device, tiles)),
            dma((per_device, tiles)),
            dma((per_device, tiles)),
            dma((per_device, tiles)),
        ],
        compiler_params=pltpu.CompilerParams(
            collective_id=1, has_side_effects=True, vmem_limit_bytes=VMEM_BYTES
        ),
        name="cross_block",
    )(lists.reshape(-1), counts.reshape(-1), hidden, wq, wk, wv, wo)


def time_block(cycle, tiles, middle, wq, wk, wv, wo):
    per_device, _, rows, channels = middle.shape
    width = wq.shape[0]
    frames = per_device * cycle // CAMS
    cells = TOKENS // frames
    kind = jnp.bfloat16
    dma = pltpu.SemaphoreType.DMA
    return pl.pallas_call(
        functools.partial(time_kernel, cycle, tiles),
        out_shape=jax.ShapeDtypeStruct((per_device, rows, channels), kind),
        in_specs=vmem(5),
        out_specs=pl.BlockSpec(memory_space=pltpu.VMEM),
        scratch_shapes=[
            pltpu.VMEM((per_device, frames, 3, cells, width), kind),
            pltpu.VMEM((per_device, frames, 3, cells, width), kind),
            pltpu.VMEM((per_device, frames, cells, width), kind),
            pltpu.VMEM((per_device, frames, cells, width), kind),
            pltpu.VMEM((per_device, tiles, rows, channels), kind),
            pltpu.VMEM((per_device, tiles, rows, channels), kind),
            pltpu.VMEM((frames * cells, width), jnp.float32),
            dma((per_device, frames)),
            dma((per_device, frames)),
            dma((per_device, frames)),
            dma((per_device, frames)),
            dma((per_device, tiles)),
            dma((per_device, tiles)),
        ],
        compiler_params=pltpu.CompilerParams(
            collective_id=2, has_side_effects=True, vmem_limit_bytes=VMEM_BYTES
        ),
        name="time_block",
    )(middle, wq, wk, wv, wo)


def on_device(
    latents, norm_gain, norm_shift, conv_weight,
    cross_query, cross_key, cross_value, cross_out,
    time_query, time_key, time_value, time_out,
    patch_lists, patch_counts,
):
    per_device, share_rows = latents.shape[:2]
    channels = latents.shape[3]
    cycle = lax.axis_size("camframe")
    tiles = lax.axis_size("tile")
    local_width = conv_weight.shape[2]
    hidden = conv_block(
        tiles, latents.reshape(per_device, share_rows * WW, channels),
        norm_gain.reshape(1, channels), norm_shift.reshape(1, channels),
        conv_weight.reshape(9, local_width, channels),
    )
    hidden = hidden.reshape(per_device, tiles, share_rows * WW, channels)
    middle = cross_block(
        cycle, tiles, patch_lists, patch_counts, hidden,
        cross_query, cross_key, cross_value, cross_out,
    )
    blended = time_block(cycle, tiles, middle, time_query, time_key, time_value, time_out)
    return blended.reshape(latents.shape)


def solution(mesh):
    return jax.shard_map(
        on_device,
        mesh=mesh,
        in_specs=(
            P("camframe", "tile", None, None),
            P(),
            P(),
            P(None, None, "tile", None),
            P("tile", None),
            P("tile", None),
            P("tile", None),
            P("tile", None),
            P("tile", None),
            P("tile", None),
            P("tile", None),
            P("tile", None),
            P(),
            P(),
        ),
        out_specs=P("camframe", "tile", None, None),
        check_vma=False,
    )
```

```python
import functools

import jax
import jax.numpy as jnp
from jax import lax
from jax.experimental import pallas as pl
from jax.experimental.pallas import tpu as pltpu
from jax.sharding import PartitionSpec as P

GROUPS = 32
CAMS = 6
HH = 16
WW = 8
PATCH = 32
P_SIZE = 2
HEAD = 160
NPATCH = 4
TOKENS = HH * WW

EPSILON = 1e-05
MESH = pl.DeviceIdType.MESH
VMEM_BYTES = 58 * 1024 * 1024


def right_product(left, weight):
    return lax.dot_general(
        left, weight, (((1,), (1,)), ((), ())), preferred_element_type=jnp.float32
    )


def layer_norm(values):
    average = jnp.mean(values, axis=-1, keepdims=True)
    centred = values - average
    spread = jnp.mean(jnp.square(centred), axis=-1, keepdims=True)
    return (centred * lax.rsqrt(spread + EPSILON)).astype(jnp.bfloat16)


def head_windows(width):
    windows = []
    for head in range(width // HEAD):
        first, last = head * HEAD, (head + 1) * HEAD
        low = first // 128 * 128
        high = min(width, -(-last // 128) * 128)
        windows.append((first, last, low, high))
    return windows


def masked_attention(queries, keys, values, keep, mixture):
    width = queries.shape[1]
    mixture[...] = jnp.zeros_like(mixture)
    for first, last, low, high in head_windows(width):
        lane = lax.broadcasted_iota(jnp.int32, (1, high - low), 1) + low
        inside = (lane >= first) & (lane < last)
        own_queries = jnp.where(inside, queries[:, low:high], jnp.bfloat16(0))
        own_values = jnp.where(inside, values[:, low:high], jnp.bfloat16(0))
        scores = right_product(own_queries, keys[:, low:high]) * HEAD ** (-0.5)
        scores = jnp.where(keep, scores, -jnp.inf)
        highest = jnp.max(scores, axis=-1, keepdims=True)
        weights = jnp.exp(scores - highest)
        weights = (weights / jnp.sum(weights, axis=-1, keepdims=True)).astype(jnp.bfloat16)
        mixture[:, low:high] += jnp.dot(
            weights, own_values, preferred_element_type=jnp.float32
        )
    return mixture[...].astype(jnp.bfloat16)


def group_sums(row, members):
    high = row.astype(jnp.bfloat16).astype(jnp.float32)
    middle = (row - high).astype(jnp.bfloat16).astype(jnp.float32)
    low = row - high - middle
    place = lax.broadcasted_iota(jnp.int32, (16, row.shape[1]), 0)
    parts = jnp.where(
        place == 0, high, jnp.where(place == 1, middle, jnp.where(place == 2, low, 0.0))
    ).astype(jnp.bfloat16)
    sums = jnp.dot(parts, members, preferred_element_type=jnp.float32)
    return jnp.sum(sums, axis=0, keepdims=True)


def scatter(me, tile, tiles, position, part, arrived, send_sem, recv_sem):
    started = []
    for other in range(1, tiles):
        target = lax.rem(tile + other, tiles)
        copy = pltpu.make_async_remote_copy(
            src_ref=part.at[position, target],
            dst_ref=arrived.at[position, other],
            send_sem=send_sem.at[position, other],
            recv_sem=recv_sem.at[position, other],
            device_id=(me, target),
            device_id_type=MESH,
        )
        copy.start()
        started.append(copy)
    return started


def gather_sum(tile, tiles, position, part, arrived, sent):
    for copy in sent:
        copy.wait()
    total = part[position, tile].astype(jnp.float32)
    for other in range(1, tiles):
        total = total + arrived[position, other].astype(jnp.float32)
    return total


def block_kernel(
    cycle, tiles, lists_ref, counts_ref, latents_ref, gain_ref, shift_ref, conv_ref,
    cq_ref, ck_ref, cv_ref, co_ref, tq_ref, tk_ref, tv_ref, to_ref,
    out_ref,
    whole, windows, conv_weights, gathered, total, matrices,
    query_buf, kv_buf, send_buf, context, part, arrived, mixture, middle,
    local, received, mixed, returned, time_part, time_arrived,
    conv_sem, matrix_sem, in_send, in_recv, out_send, out_recv,
    kv_send, kv_recv, rs_send, rs_recv, ag_send, ag_recv,
    qkv_send, qkv_recv, mix_send, mix_recv, rt_send, rt_recv,
):
    per_device, rows, channels = latents_ref.shape
    taps, width = conv_ref.shape[:2]
    views = per_device * cycle
    frames = views // CAMS
    cells = TOKENS // frames
    me = lax.axis_index("camframe")
    tile = lax.axis_index("tile")

    def load(tap):
        return pltpu.make_async_copy(
            conv_ref.at[tap], conv_weights.at[tap], conv_sem.at[tap]
        )

    loads = [
        pltpu.make_async_copy(ref, matrices.at[index], matrix_sem.at[index])
        for index, ref in enumerate(
            (cq_ref, ck_ref, cv_ref, co_ref, tq_ref, tk_ref, tv_ref, to_ref)
        )
    ]
    loaded = set()

    def matrix(index):
        if index not in loaded:
            loads[index].wait()
            loaded.add(index)
        return matrices[index]

    for tap in range(taps):
        load(tap).start()
    steps = [
        (side, position, (frames, -frames)[side])
        for side in range(2)
        for position in range(per_device)
    ]
    offsets = sorted({((position + step) // per_device) % cycle for _, position, step in steps})
    first_camera = per_device * me // frames
    last_camera = (per_device * me + per_device - 1) // frames
    reach = (frames - 1 + per_device - 1) // per_device
    barrier = pltpu.get_barrier_semaphore()

    def is_peer(offset):
        other = me + offset
        other_first = (per_device * (other + cycle)) // frames - CAMS
        other_last = (per_device * (other + cycle) + per_device - 1) // frames - CAMS
        return (other >= 0) & (other < cycle) & (other_first <= last_camera) & (first_camera <= other_last)

    peers = len(offsets) + tiles - 1
    for offset in offsets:
        pl.semaphore_signal(
            barrier, inc=1, device_id=(lax.rem(me + offset, cycle), tile), device_id_type=MESH
        )
    for offset in range(-reach, reach + 1):
        if offset != 0:
            peers = peers + jnp.where(is_peer(offset), 1, 0)

            @pl.when(is_peer(offset))
            def _():
                pl.semaphore_signal(
                    barrier, inc=1, device_id=(me + offset, tile), device_id_type=MESH
                )
    for other in range(1, tiles):
        pl.semaphore_signal(
            barrier, inc=1, device_id=(me, lax.rem(tile + other, tiles)), device_id_type=MESH
        )
    pl.semaphore_wait(barrier, peers)

    def to_others(source, target, send_sem, recv_sem, position):
        started = []
        for other in range(1, tiles):
            copy = pltpu.make_async_remote_copy(
                src_ref=source,
                dst_ref=target,
                send_sem=send_sem.at[position, other],
                recv_sem=recv_sem.at[position, other],
                device_id=(me, lax.rem(tile + other, tiles)),
                device_id_type=MESH,
            )
            copy.start()
            started.append(copy)
        return started

    incoming = [
        to_others(
            latents_ref.at[position], whole.at[position, tile], in_send, in_recv, position
        )
        for position in range(per_device)
    ]
    for copy in loads:
        copy.start()
    size = channels // GROUPS
    shape = (channels, 128)
    members = (
        lax.broadcasted_iota(jnp.int32, shape, 0) // size
        == lax.broadcasted_iota(jnp.int32, shape, 1)
    ).astype(jnp.float32).astype(jnp.bfloat16)
    shape = (128, channels)
    spread_out = (
        lax.broadcasted_iota(jnp.int32, shape, 1) // size
        == lax.broadcasted_iota(jnp.int32, shape, 0)
    ).astype(jnp.float32).astype(jnp.bfloat16)
    column = lax.rem(lax.broadcasted_iota(jnp.int32, (TOKENS, 1), 0), WW)

    def group_mean(row):
        return group_sums(group_sums(row, members) / size, spread_out)

    def prepare(position):
        whole[position, tile] = latents_ref[position]
        for copy in incoming[position]:
            copy.wait()
        values = whole[position].reshape(TOKENS, channels).astype(jnp.float32)
        channel_mean = jnp.mean(values, axis=0, keepdims=True)
        average = group_mean(channel_mean)
        centred = values - average
        spread = group_mean(jnp.mean(jnp.square(centred), axis=0, keepdims=True))
        normed = centred * lax.rsqrt(spread + EPSILON)
        activated = jax.nn.silu(normed * gain_ref[...].reshape(1, channels) + shift_ref[...].reshape(1, channels))
        empty_row = jnp.zeros((1, channels), jnp.float32)
        empty = jnp.zeros((WW, channels), jnp.float32)
        for col_shift in range(3):
            if col_shift == 0:
                moved = jnp.concatenate([empty_row, activated[:-1]], axis=0)
                moved = jnp.where(column == 0, 0.0, moved)
            elif col_shift == 2:
                moved = jnp.concatenate([activated[1:], empty_row], axis=0)
                moved = jnp.where(column == WW - 1, 0.0, moved)
            else:
                moved = activated
            windows[col_shift] = jnp.concatenate(
                [empty, moved[:-WW]], axis=0
            ).astype(jnp.bfloat16)
            windows[3 + col_shift] = moved.astype(jnp.bfloat16)
            windows[6 + col_shift] = jnp.concatenate(
                [moved[WW:], empty], axis=0
            ).astype(jnp.bfloat16)

    def convolve(position):
        prepare(position)
        total[...] = jnp.zeros_like(total)

        def add(tap, carry):
            if position == 0:
                load(tap).wait()
            total[...] += right_product(windows[tap], conv_weights[tap])
            return carry

        lax.fori_loop(0, taps, add, 0)
        residual = jnp.zeros((TOKENS, width), jnp.float32)
        for piece in range(tiles):
            share = whole[position, :, :, piece * width : (piece + 1) * width]
            share = share.reshape(TOKENS, width).astype(jnp.float32)
            residual = jnp.where(tile == piece, share, residual)
        gathered[position, tile] = (residual + total[...]).astype(jnp.bfloat16)
        return to_others(
            gathered.at[position, tile], gathered.at[position, tile],
            out_send, out_recv, position,
        )

    copies = {}

    def share_context(position, outgoing):
        for copy in outgoing:
            copy.wait()
        for piece in range(tiles):
            whole[position, :, :, piece * width : (piece + 1) * width] = gathered[
                position, piece
            ].reshape(tiles, rows, width)
        normed = layer_norm(whole[position].reshape(TOKENS, channels).astype(jnp.float32))
        block = (NPATCH, PATCH, width)
        for which in range(2):
            kv_buf[position, :, which] = (
                right_product(normed, matrix(1 + which)).astype(jnp.bfloat16).reshape(block)
            )
        for side in range(2):
            step = (frames, -frames)[side]
            target_view = lax.rem(per_device * me + position + step + views, views)
            camera = target_view // frames
            for slot in range(P_SIZE):
                chosen = lists_ref[camera, side, slot]
                send_buf[position, side, slot] = kv_buf[position, chosen]
            target = lax.rem(me + ((position + step) // per_device) % cycle, cycle)
            target_slot = (position + step) % per_device
            copy = pltpu.make_async_remote_copy(
                src_ref=send_buf.at[position, side],
                dst_ref=context.at[target_slot, side],
                send_sem=kv_send.at[position, side],
                recv_sem=kv_recv.at[target_slot, side],
                device_id=(target, tile),
                device_id_type=MESH,
            )
            copy.start()
            copies[target_slot, side] = copy
        query_buf[position] = right_product(normed, matrix(0)).astype(jnp.bfloat16)

    pending = None
    for position in range(per_device):
        outgoing = convolve(position)
        if pending is not None:
            share_context(*pending)
        pending = (position, outgoing)
    share_context(*pending)

    def attend(position):
        copies[position, 0].wait_recv()
        copies[position, 1].wait_recv()
        camera = (per_device * me + position) // frames
        place = lax.broadcasted_iota(jnp.int32, (1, 2 * P_SIZE * PATCH), 1) // PATCH
        count = jnp.where(place < P_SIZE, counts_ref[camera, 0], counts_ref[camera, 1])
        live = lax.rem(place, P_SIZE) < count
        keys = context[position, :, :, 0].reshape(2 * P_SIZE * PATCH, width)
        values = context[position, :, :, 1].reshape(2 * P_SIZE * PATCH, width)
        result = masked_attention(query_buf[position], keys, values, live, mixture)
        product = jnp.dot(result, matrix(3), preferred_element_type=jnp.float32)
        part[position] = product.astype(jnp.bfloat16).reshape(tiles, rows, channels)
        return scatter(me, tile, tiles, position, part, arrived, rs_send, rs_recv)

    def finish(position, sent):
        added = gather_sum(tile, tiles, position, part, arrived, sent)
        own = whole[position, tile].astype(jnp.float32) + added
        middle[position, tile] = own.astype(jnp.bfloat16)
        return to_others(
            middle.at[position, tile], middle.at[position, tile], ag_send, ag_recv, position
        )

    def transpose(source, target, send_sem, recv_sem, slot, group, action):
        unit = per_device * me + slot
        camera, frame = unit // frames, lax.rem(unit, frames)
        goal = camera * frames + group
        goal_device, goal_slot = goal // per_device, lax.rem(goal, per_device)
        remote = pltpu.make_async_remote_copy(
            src_ref=source.at[slot, group],
            dst_ref=target.at[goal_slot, frame],
            send_sem=send_sem.at[slot, group],
            recv_sem=recv_sem.at[goal_slot, frame],
            device_id=(goal_device, tile),
            device_id_type=MESH,
        )
        if action == "start":
            @pl.when(goal_device != me)
            def _():
                remote.start()

            @pl.when(goal_device == me)
            def _():
                pltpu.make_async_copy(
                    source.at[slot, group], target.at[goal_slot, frame], recv_sem.at[goal_slot, frame]
                ).start()
        else:
            @pl.when(goal_device != me)
            def _():
                remote.wait_send()

    def landed(source, target, recv_sem, slot, frame):
        pltpu.make_async_copy(
            source.at[slot, frame], target.at[slot, frame], recv_sem.at[slot, frame]
        ).wait()

    def each(slot, action):
        def body(group, carry):
            action(slot, group)
            return carry

        lax.fori_loop(0, frames, body, 0)

    def share_frames(position, outgoing):
        for copy in outgoing:
            copy.wait()
        normed = layer_norm(middle[position].reshape(TOKENS, channels).astype(jnp.float32))
        for which in range(3):
            local[position, :, which] = (
                right_product(normed, matrix(4 + which))
                .astype(jnp.bfloat16)
                .reshape(frames, cells, width)
            )
        each(
            position,
            lambda s, g: transpose(local, received, qkv_send, qkv_recv, s, g, "start"),
        )

    order = sorted(
        range(per_device),
        key=lambda r: max((r - frames) % per_device, (r + frames) % per_device),
    )
    attended, finished = [], []
    for position in order:
        attended.append((position, attend(position)))
        if len(attended) > 1:
            earlier, sent = attended[-2]
            finished.append((earlier, finish(earlier, sent)))
        if len(finished) > 1:
            share_frames(*finished[-2])
    last, sent = attended[-1]
    finished.append((last, finish(last, sent)))
    for entry in finished[max(len(finished) - 2, 0) :]:
        share_frames(*entry)
    tokens_in = frames * cells
    row_cell = lax.rem(lax.broadcasted_iota(jnp.int32, (tokens_in, tokens_in), 0), cells)
    column_cell = lax.rem(lax.broadcasted_iota(jnp.int32, (tokens_in, tokens_in), 1), cells)
    keep = row_cell == column_cell
    for slot in range(per_device):
        each(slot, lambda s, g: landed(local, received, qkv_recv, s, g))
        queries, keys, values = (
            received[slot, :, which].reshape(tokens_in, width) for which in range(3)
        )
        result = masked_attention(queries, keys, values, keep, mixture)
        mixed[slot] = result.reshape(frames, cells, width)
        each(slot, lambda s, g: transpose(mixed, returned, mix_send, mix_recv, s, g, "start"))
    sent = []
    for slot in range(per_device):
        each(slot, lambda s, g: landed(mixed, returned, mix_recv, s, g))
        total = jnp.dot(
            returned[slot].reshape(TOKENS, width), matrix(7), preferred_element_type=jnp.float32
        )
        time_part[slot] = total.astype(jnp.bfloat16).reshape(tiles, rows, channels)
        sent.append(scatter(me, tile, tiles, slot, time_part, time_arrived, rt_send, rt_recv))
    for slot in range(per_device):
        total = gather_sum(tile, tiles, slot, time_part, time_arrived, sent[slot])
        own = middle[slot, tile].astype(jnp.float32) + total
        out_ref[slot] = own.astype(jnp.bfloat16)
    for slot in range(per_device):
        each(slot, lambda s, g: transpose(local, received, qkv_send, qkv_recv, s, g, "wait"))
        each(slot, lambda s, g: transpose(mixed, returned, mix_send, mix_recv, s, g, "wait"))


    for copy in copies.values():
        copy.wait_send()


def whole_block(cycle, tiles, lists, counts, latents, gain, shift, conv_weight, *matrices):
    per_device, rows, channels = latents.shape
    taps, width = conv_weight.shape[:2]
    frames = per_device * cycle // CAMS
    cells = TOKENS // frames
    kind = jnp.bfloat16
    dma = pltpu.SemaphoreType.DMA
    by_tile = dma((per_device, tiles))
    by_frame = dma((per_device, frames))
    vmem = pl.BlockSpec(memory_space=pltpu.VMEM)
    smem = pl.BlockSpec(memory_space=pltpu.SMEM)
    shares = pltpu.VMEM((per_device, tiles, rows, channels), kind)
    patches = pltpu.VMEM((per_device, 2, P_SIZE, 2, PATCH, width), kind)
    return pl.pallas_call(
        functools.partial(block_kernel, cycle, tiles),
        out_shape=jax.ShapeDtypeStruct((per_device, rows, channels), kind),
        in_specs=[smem] * 2 + [vmem] * 3 + [pl.BlockSpec(memory_space=pl.ANY)] * 9,
        out_specs=vmem,
        scratch_shapes=[
            shares,
            pltpu.VMEM((taps, TOKENS, channels), kind),
            pltpu.VMEM((taps, width, channels), kind),
            pltpu.VMEM((per_device, tiles, TOKENS, width), kind),
            pltpu.VMEM((TOKENS, width), jnp.float32),
            pltpu.VMEM((8, width, channels), kind),
            pltpu.VMEM((per_device, TOKENS, width), kind),
            pltpu.VMEM((per_device, NPATCH, 2, PATCH, width), kind),
            patches,
            patches,
            shares,
            shares,
            pltpu.VMEM((TOKENS, width), jnp.float32),
            shares,
            pltpu.VMEM((per_device, frames, 3, cells, width), kind),
            pltpu.VMEM((per_device, frames, 3, cells, width), kind),
            pltpu.VMEM((per_device, frames, cells, width), kind),
            pltpu.VMEM((per_device, frames, cells, width), kind),
            shares,
            shares,
            dma((taps,)),
            dma((8,)),
            by_tile, by_tile, by_tile, by_tile,
            dma((per_device, 2)),
            dma((per_device, 2)),
            by_tile, by_tile, by_tile, by_tile,
            by_frame, by_frame, by_frame, by_frame,
            by_tile, by_tile,
        ],
        compiler_params=pltpu.CompilerParams(
            collective_id=1, has_side_effects=True, vmem_limit_bytes=VMEM_BYTES
        ),
        name="whole_block",
    )(lists, counts, latents, gain, shift, conv_weight, *matrices)


def on_device(
    latents, norm_gain, norm_shift, conv_weight,
    cross_query, cross_key, cross_value, cross_out,
    time_query, time_key, time_value, time_out,
    patch_lists, patch_counts,
):
    per_device, share_rows, _, channels = latents.shape
    blended = whole_block(
        lax.axis_size("camframe"), lax.axis_size("tile"), patch_lists, patch_counts,
        latents.reshape(per_device, share_rows * WW, channels),
        norm_gain, norm_shift, conv_weight.reshape(9, -1, channels),
        cross_query, cross_key, cross_value, cross_out,
        time_query, time_key, time_value, time_out,
    )
    return blended.reshape(latents.shape)


def solution(mesh):
    return jax.shard_map(
        on_device,
        mesh=mesh,
        in_specs=(
            P("camframe", "tile", None, None),
            P(),
            P(),
            P(None, None, "tile", None),
            P("tile", None),
            P("tile", None),
            P("tile", None),
            P("tile", None),
            P("tile", None),
            P("tile", None),
            P("tile", None),
            P("tile", None),
            P(),
            P(),
        ),
        out_specs=P("camframe", "tile", None, None),
        check_vma=False,
    )
```

```python
import functools

import jax
import jax.numpy as jnp
from jax import lax
from jax.experimental import pallas as pl
from jax.experimental.pallas import tpu as pltpu
from jax.sharding import PartitionSpec as P

GROUPS = 32
CAMS = 6
HH = 16
WW = 8
PATCH = 32
P_SIZE = 2
HEAD = 160
NPATCH = 4
TOKENS = HH * WW

EPSILON = 1e-05
MESH = pl.DeviceIdType.MESH
VMEM_BYTES = 50 * 1024 * 1024


def right_product(left, weight):
    return lax.dot_general(
        left, weight, (((1,), (1,)), ((), ())), preferred_element_type=jnp.float32
    )


def layer_norm(values):
    average = jnp.mean(values, axis=-1, keepdims=True)
    centred = values - average
    spread = jnp.mean(jnp.square(centred), axis=-1, keepdims=True)
    return (centred * lax.rsqrt(spread + EPSILON)).astype(jnp.bfloat16)


def head_windows(width):
    windows = []
    for head in range(width // HEAD):
        first, last = head * HEAD, (head + 1) * HEAD
        low = first // 128 * 128
        high = min(width, -(-last // 128) * 128)
        windows.append((first, last, low, high))
    return windows


def masked_attention(queries, keys, values, keep, mixture):
    width = queries.shape[1]
    mixture[...] = jnp.zeros_like(mixture)
    for first, last, low, high in head_windows(width):
        lane = lax.broadcasted_iota(jnp.int32, (1, high - low), 1) + low
        inside = (lane >= first) & (lane < last)
        own_queries = jnp.where(inside, queries[:, low:high], jnp.bfloat16(0))
        own_values = jnp.where(inside, values[:, low:high], jnp.bfloat16(0))
        scores = right_product(own_queries, keys[:, low:high]) * HEAD ** (-0.5)
        scores = jnp.where(keep, scores, -jnp.inf)
        highest = jnp.max(scores, axis=-1, keepdims=True)
        weights = jnp.exp(scores - highest)
        weights = (weights / jnp.sum(weights, axis=-1, keepdims=True)).astype(jnp.bfloat16)
        mixture[:, low:high] += jnp.dot(
            weights, own_values, preferred_element_type=jnp.float32
        )
    return mixture[...].astype(jnp.bfloat16)


def group_sums(row, members):
    high = row.astype(jnp.bfloat16).astype(jnp.float32)
    middle = (row - high).astype(jnp.bfloat16).astype(jnp.float32)
    low = row - high - middle
    place = lax.broadcasted_iota(jnp.int32, (16, row.shape[1]), 0)
    parts = jnp.where(
        place == 0, high, jnp.where(place == 1, middle, jnp.where(place == 2, low, 0.0))
    ).astype(jnp.bfloat16)
    sums = jnp.dot(parts, members, preferred_element_type=jnp.float32)
    return jnp.sum(sums, axis=0, keepdims=True)


def scatter(me, tile, tiles, position, part, arrived, send_sem, recv_sem):
    started = []
    for other in range(1, tiles):
        target = lax.rem(tile + other, tiles)
        copy = pltpu.make_async_remote_copy(
            src_ref=part.at[position, target],
            dst_ref=arrived.at[position, other],
            send_sem=send_sem.at[position, other],
            recv_sem=recv_sem.at[position, other],
            device_id=(me, target),
            device_id_type=MESH,
        )
        copy.start()
        started.append(copy)
    return started


def gather_sum(tile, tiles, position, part, arrived, sent):
    for copy in sent:
        copy.wait()
    total = part[position, tile].astype(jnp.float32)
    for other in range(1, tiles):
        total = total + arrived[position, other].astype(jnp.float32)
    return total


def block_kernel(
    cycle, tiles, lists_ref, counts_ref, latents_ref, gain_ref, shift_ref, conv_ref,
    cq_ref, ck_ref, cv_ref, co_ref, tq_ref, tk_ref, tv_ref, to_ref,
    out_ref,
    whole, windows, conv_weights, gathered, total, matrices,
    query_buf, kv_buf, send_buf, context, part, arrived, mixture, middle,
    local, received, mixed, returned, time_part, time_arrived,
    conv_sem, matrix_sem, in_send, in_recv, out_send, out_recv,
    kv_send, kv_recv, rs_send, rs_recv, ag_send, ag_recv,
    qkv_send, qkv_recv, mix_send, mix_recv, rt_send, rt_recv,
):
    per_device, rows, channels = latents_ref.shape
    taps, width = conv_ref.shape[:2]
    views = per_device * cycle
    frames = views // CAMS
    cells = TOKENS // frames
    me = lax.axis_index("camframe")
    tile = lax.axis_index("tile")

    def load(tap):
        return pltpu.make_async_copy(
            conv_ref.at[tap], conv_weights.at[tap], conv_sem.at[tap]
        )

    loads = [
        pltpu.make_async_copy(ref, matrices.at[index], matrix_sem.at[index])
        for index, ref in enumerate(
            (cq_ref, ck_ref, cv_ref, co_ref, tq_ref, tk_ref, tv_ref, to_ref)
        )
    ]
    loaded = set()

    def matrix(index):
        if index not in loaded:
            loads[index].wait()
            loaded.add(index)
        return matrices[index]

    for tap in range(taps):
        load(tap).start()
    steps = [
        (side, position, (frames, -frames)[side])
        for side in range(2)
        for position in range(per_device)
    ]
    offsets = sorted({((position + step) // per_device) % cycle for _, position, step in steps})
    first_camera = per_device * me // frames
    last_camera = (per_device * me + per_device - 1) // frames
    reach = (frames - 1 + per_device - 1) // per_device
    barrier = pltpu.get_barrier_semaphore()

    def is_peer(offset):
        other = me + offset
        other_first = (per_device * (other + cycle)) // frames - CAMS
        other_last = (per_device * (other + cycle) + per_device - 1) // frames - CAMS
        return (other >= 0) & (other < cycle) & (other_first <= last_camera) & (first_camera <= other_last)

    peers = len(offsets) + tiles - 1
    for offset in offsets:
        pl.semaphore_signal(
            barrier, inc=1, device_id=(lax.rem(me + offset, cycle), tile), device_id_type=MESH
        )
    for offset in range(-reach, reach + 1):
        if offset != 0:
            peers = peers + jnp.where(is_peer(offset), 1, 0)

            @pl.when(is_peer(offset))
            def _():
                pl.semaphore_signal(
                    barrier, inc=1, device_id=(me + offset, tile), device_id_type=MESH
                )
    for other in range(1, tiles):
        pl.semaphore_signal(
            barrier, inc=1, device_id=(me, lax.rem(tile + other, tiles)), device_id_type=MESH
        )
    pl.semaphore_wait(barrier, peers)

    def to_others(source, target, send_sem, recv_sem, position):
        started = []
        for other in range(1, tiles):
            copy = pltpu.make_async_remote_copy(
                src_ref=source,
                dst_ref=target,
                send_sem=send_sem.at[position, other],
                recv_sem=recv_sem.at[position, other],
                device_id=(me, lax.rem(tile + other, tiles)),
                device_id_type=MESH,
            )
            copy.start()
            started.append(copy)
        return started

    incoming = [
        to_others(
            latents_ref.at[position], whole.at[position, tile], in_send, in_recv, position
        )
        for position in range(per_device)
    ]
    for copy in loads:
        copy.start()
    size = channels // GROUPS
    shape = (channels, 128)
    members = (
        lax.broadcasted_iota(jnp.int32, shape, 0) // size
        == lax.broadcasted_iota(jnp.int32, shape, 1)
    ).astype(jnp.float32).astype(jnp.bfloat16)
    shape = (128, channels)
    spread_out = (
        lax.broadcasted_iota(jnp.int32, shape, 1) // size
        == lax.broadcasted_iota(jnp.int32, shape, 0)
    ).astype(jnp.float32).astype(jnp.bfloat16)
    column = lax.rem(lax.broadcasted_iota(jnp.int32, (TOKENS, 1), 0), WW)

    def group_mean(row):
        return group_sums(group_sums(row, members) / size, spread_out)

    def prepare(position):
        whole[position, tile] = latents_ref[position]
        for copy in incoming[position]:
            copy.wait()
        values = whole[position].reshape(TOKENS, channels).astype(jnp.float32)
        channel_mean = jnp.mean(values, axis=0, keepdims=True)
        average = group_mean(channel_mean)
        centred = values - average
        spread = group_mean(jnp.mean(jnp.square(centred), axis=0, keepdims=True))
        normed = centred * lax.rsqrt(spread + EPSILON)
        activated = jax.nn.silu(normed * gain_ref[...].reshape(1, channels) + shift_ref[...].reshape(1, channels))
        empty_row = jnp.zeros((1, channels), jnp.float32)
        empty = jnp.zeros((WW, channels), jnp.float32)
        for col_shift in range(3):
            if col_shift == 0:
                moved = jnp.concatenate([empty_row, activated[:-1]], axis=0)
                moved = jnp.where(column == 0, 0.0, moved)
            elif col_shift == 2:
                moved = jnp.concatenate([activated[1:], empty_row], axis=0)
                moved = jnp.where(column == WW - 1, 0.0, moved)
            else:
                moved = activated
            windows[col_shift] = jnp.concatenate(
                [empty, moved[:-WW]], axis=0
            ).astype(jnp.bfloat16)
            windows[3 + col_shift] = moved.astype(jnp.bfloat16)
            windows[6 + col_shift] = jnp.concatenate(
                [moved[WW:], empty], axis=0
            ).astype(jnp.bfloat16)

    def convolve(position):
        prepare(position)
        total[...] = jnp.zeros_like(total)

        def add(tap, carry):
            if position == 0:
                load(tap).wait()
            total[...] += right_product(windows[tap], conv_weights[tap])
            return carry

        lax.fori_loop(0, taps, add, 0)
        residual = jnp.zeros((TOKENS, width), jnp.float32)
        for piece in range(tiles):
            share = whole[position, :, :, piece * width : (piece + 1) * width]
            share = share.reshape(TOKENS, width).astype(jnp.float32)
            residual = jnp.where(tile == piece, share, residual)
        gathered[position, tile] = (residual + total[...]).astype(jnp.bfloat16)
        return to_others(
            gathered.at[position, tile], gathered.at[position, tile],
            out_send, out_recv, position,
        )

    copies = {}

    def share_context(position, outgoing):
        for copy in outgoing:
            copy.wait()
        for piece in range(tiles):
            whole[position, :, :, piece * width : (piece + 1) * width] = gathered[
                position, piece
            ].reshape(tiles, rows, width)
        normed = layer_norm(whole[position].reshape(TOKENS, channels).astype(jnp.float32))
        block = (NPATCH, PATCH, width)
        for which in range(2):
            kv_buf[position, :, which] = (
                right_product(normed, matrix(1 + which)).astype(jnp.bfloat16).reshape(block)
            )
        for side in range(2):
            step = (frames, -frames)[side]
            target_view = lax.rem(per_device * me + position + step + views, views)
            camera = target_view // frames
            for slot in range(P_SIZE):
                chosen = lists_ref[camera, side, slot]
                send_buf[position, side, slot] = kv_buf[position, chosen]
            target = lax.rem(me + ((position + step) // per_device) % cycle, cycle)
            target_slot = (position + step) % per_device
            copy = pltpu.make_async_remote_copy(
                src_ref=send_buf.at[position, side],
                dst_ref=context.at[target_slot, side],
                send_sem=kv_send.at[position, side],
                recv_sem=kv_recv.at[target_slot, side],
                device_id=(target, tile),
                device_id_type=MESH,
            )
            copy.start()
            copies[target_slot, side] = copy
        query_buf[position] = right_product(normed, matrix(0)).astype(jnp.bfloat16)

    pending = None
    for position in range(per_device):
        outgoing = convolve(position)
        if pending is not None:
            share_context(*pending)
        pending = (position, outgoing)
    share_context(*pending)

    def attend(position):
        copies[position, 0].wait_recv()
        copies[position, 1].wait_recv()
        camera = (per_device * me + position) // frames
        place = lax.broadcasted_iota(jnp.int32, (1, 2 * P_SIZE * PATCH), 1) // PATCH
        count = jnp.where(place < P_SIZE, counts_ref[camera, 0], counts_ref[camera, 1])
        live = lax.rem(place, P_SIZE) < count
        keys = context[position, :, :, 0].reshape(2 * P_SIZE * PATCH, width)
        values = context[position, :, :, 1].reshape(2 * P_SIZE * PATCH, width)
        result = masked_attention(query_buf[position], keys, values, live, mixture)
        product = jnp.dot(result, matrix(3), preferred_element_type=jnp.float32)
        part[position] = product.astype(jnp.bfloat16).reshape(tiles, rows, channels)
        return scatter(me, tile, tiles, position, part, arrived, rs_send, rs_recv)

    def finish(position, sent):
        added = gather_sum(tile, tiles, position, part, arrived, sent)
        own = whole[position, tile].astype(jnp.float32) + added
        middle[position, tile] = own.astype(jnp.bfloat16)
        return to_others(
            middle.at[position, tile], middle.at[position, tile], ag_send, ag_recv, position
        )

    def transpose(source, target, send_sem, recv_sem, slot, group, action):
        unit = per_device * me + slot
        camera, frame = unit // frames, lax.rem(unit, frames)
        goal = camera * frames + group
        goal_device, goal_slot = goal // per_device, lax.rem(goal, per_device)
        remote = pltpu.make_async_remote_copy(
            src_ref=source.at[slot, group],
            dst_ref=target.at[goal_slot, frame],
            send_sem=send_sem.at[slot, group],
            recv_sem=recv_sem.at[goal_slot, frame],
            device_id=(goal_device, tile),
            device_id_type=MESH,
        )
        if action == "start":
            @pl.when(goal_device != me)
            def _():
                remote.start()

            @pl.when(goal_device == me)
            def _():
                pltpu.make_async_copy(
                    source.at[slot, group], target.at[goal_slot, frame], recv_sem.at[goal_slot, frame]
                ).start()
        else:
            @pl.when(goal_device != me)
            def _():
                remote.wait_send()

    def landed(source, target, recv_sem, slot, frame):
        pltpu.make_async_copy(
            source.at[slot, frame], target.at[slot, frame], recv_sem.at[slot, frame]
        ).wait()

    def each(slot, action):
        def body(group, carry):
            action(slot, group)
            return carry

        lax.fori_loop(0, frames, body, 0)

    def share_frames(position, outgoing):
        for copy in outgoing:
            copy.wait()
        normed = layer_norm(middle[position].reshape(TOKENS, channels).astype(jnp.float32))
        for which in range(3):
            local[position, :, which] = (
                right_product(normed, matrix(4 + which))
                .astype(jnp.bfloat16)
                .reshape(frames, cells, width)
            )
        each(
            position,
            lambda s, g: transpose(local, received, qkv_send, qkv_recv, s, g, "start"),
        )

    order = sorted(
        range(per_device),
        key=lambda r: max((r - frames) % per_device, (r + frames) % per_device),
    )
    attended, finished = [], []
    for position in order:
        attended.append((position, attend(position)))
        if len(attended) > 1:
            earlier, sent = attended[-2]
            finished.append((earlier, finish(earlier, sent)))
        if len(finished) > 1:
            share_frames(*finished[-2])
    last, sent = attended[-1]
    finished.append((last, finish(last, sent)))
    for entry in finished[max(len(finished) - 2, 0) :]:
        share_frames(*entry)
    tokens_in = frames * cells
    row_cell = lax.rem(lax.broadcasted_iota(jnp.int32, (tokens_in, tokens_in), 0), cells)
    column_cell = lax.rem(lax.broadcasted_iota(jnp.int32, (tokens_in, tokens_in), 1), cells)
    keep = row_cell == column_cell
    for slot in range(per_device):
        each(slot, lambda s, g: landed(local, received, qkv_recv, s, g))
        queries, keys, values = (
            received[slot, :, which].reshape(tokens_in, width) for which in range(3)
        )
        result = masked_attention(queries, keys, values, keep, mixture)
        mixed[slot] = result.reshape(frames, cells, width)
        each(slot, lambda s, g: transpose(mixed, returned, mix_send, mix_recv, s, g, "start"))
    sent = []
    for slot in range(per_device):
        each(slot, lambda s, g: landed(mixed, returned, mix_recv, s, g))
        total = jnp.dot(
            returned[slot].reshape(TOKENS, width), matrix(7), preferred_element_type=jnp.float32
        )
        time_part[slot] = total.astype(jnp.bfloat16).reshape(tiles, rows, channels)
        sent.append(scatter(me, tile, tiles, slot, time_part, time_arrived, rt_send, rt_recv))
    for slot in range(per_device):
        total = gather_sum(tile, tiles, slot, time_part, time_arrived, sent[slot])
        own = middle[slot, tile].astype(jnp.float32) + total
        out_ref[slot] = own.astype(jnp.bfloat16)
    for slot in range(per_device):
        each(slot, lambda s, g: transpose(local, received, qkv_send, qkv_recv, s, g, "wait"))
        each(slot, lambda s, g: transpose(mixed, returned, mix_send, mix_recv, s, g, "wait"))


    for copy in copies.values():
        copy.wait_send()


def whole_block(cycle, tiles, lists, counts, latents, gain, shift, conv_weight, *matrices):
    per_device, rows, channels = latents.shape
    taps, width = conv_weight.shape[:2]
    frames = per_device * cycle // CAMS
    cells = TOKENS // frames
    kind = jnp.bfloat16
    dma = pltpu.SemaphoreType.DMA
    by_tile = dma((per_device, tiles))
    by_frame = dma((per_device, frames))
    vmem = pl.BlockSpec(memory_space=pltpu.VMEM)
    smem = pl.BlockSpec(memory_space=pltpu.SMEM)
    shares = pltpu.VMEM((per_device, tiles, rows, channels), kind)
    patches = pltpu.VMEM((per_device, 2, P_SIZE, 2, PATCH, width), kind)
    return pl.pallas_call(
        functools.partial(block_kernel, cycle, tiles),
        out_shape=jax.ShapeDtypeStruct((per_device, rows, channels), kind),
        in_specs=[smem] * 2 + [vmem] * 3 + [pl.BlockSpec(memory_space=pl.ANY)] * 9,
        out_specs=vmem,
        scratch_shapes=[
            shares,
            pltpu.VMEM((taps, TOKENS, channels), kind),
            pltpu.VMEM((taps, width, channels), kind),
            pltpu.VMEM((per_device, tiles, TOKENS, width), kind),
            pltpu.VMEM((TOKENS, width), jnp.float32),
            pltpu.VMEM((8, width, channels), kind),
            pltpu.VMEM((per_device, TOKENS, width), kind),
            pltpu.VMEM((per_device, NPATCH, 2, PATCH, width), kind),
            patches,
            patches,
            shares,
            shares,
            pltpu.VMEM((TOKENS, width), jnp.float32),
            shares,
            pltpu.VMEM((per_device, frames, 3, cells, width), kind),
            pltpu.VMEM((per_device, frames, 3, cells, width), kind),
            pltpu.VMEM((per_device, frames, cells, width), kind),
            pltpu.VMEM((per_device, frames, cells, width), kind),
            shares,
            shares,
            dma((taps,)),
            dma((8,)),
            by_tile, by_tile, by_tile, by_tile,
            dma((per_device, 2)),
            dma((per_device, 2)),
            by_tile, by_tile, by_tile, by_tile,
            by_frame, by_frame, by_frame, by_frame,
            by_tile, by_tile,
        ],
        compiler_params=pltpu.CompilerParams(
            collective_id=1, has_side_effects=True, vmem_limit_bytes=VMEM_BYTES
        ),
        name="whole_block",
    )(lists, counts, latents, gain, shift, conv_weight, *matrices)


def on_device(
    latents, norm_gain, norm_shift, conv_weight,
    cross_query, cross_key, cross_value, cross_out,
    time_query, time_key, time_value, time_out,
    patch_lists, patch_counts,
):
    per_device, share_rows, _, channels = latents.shape
    blended = whole_block(
        lax.axis_size("camframe"), lax.axis_size("tile"), patch_lists, patch_counts,
        latents.reshape(per_device, share_rows * WW, channels),
        norm_gain, norm_shift, conv_weight.reshape(9, -1, channels),
        cross_query, cross_key, cross_value, cross_out,
        time_query, time_key, time_value, time_out,
    )
    return blended.reshape(latents.shape)


def solution(mesh):
    return jax.shard_map(
        on_device,
        mesh=mesh,
        in_specs=(
            P("camframe", "tile", None, None),
            P(),
            P(),
            P(None, None, "tile", None),
            P("tile", None),
            P("tile", None),
            P("tile", None),
            P("tile", None),
            P("tile", None),
            P("tile", None),
            P("tile", None),
            P("tile", None),
            P(),
            P(),
        ),
        out_specs=P("camframe", "tile", None, None),
        check_vma=False,
    )
```
